32 devices in a mesh: seq: 8 (over y, x, core), head: 4 (over z).
Axes of the slice: x: 2, y: 2, z: 4, core: 2. Of those that a mesh axis runs over, the one named last changes fastest.
Arguments:
- queries: bfloat16 [4096, 2048], P('seq', 'head'), may hold values from -60 to 60
- keys: bfloat16 [4096, 2048], P('seq', 'head'), may hold values from -6 to 6
- values: bfloat16 [4096, 2048], P('seq', 'head'), may hold values from -6 to 6
- grad_out: bfloat16 [4096, 2048], P('seq', 'head'), may hold values from -6 to 6
- retrieved: int32 [64, 16], P(('seq', 'head')), may hold values from 0 to 63, as said below
- mem_bias: float32 [16], P('head'), may hold values from -2 to 1
Outputs:
- attended: bfloat16 [4096, 2048], P('seq', 'head')
- grad_queries: bfloat16 [4096, 2048], P('seq', 'head')
- grad_keys: bfloat16 [4096, 2048], P('seq', 'head')
- grad_values: bfloat16 [4096, 2048], P('seq', 'head')
The draws below stay inside these ranges and needn't reach their ends.
Inputs may be any that keep to these rules, and one draw needn't show every extreme that they name: `retrieved`: each row names 16 different blocks. The 8 rows of one segment name exactly 32 distinct blocks together, at most 4 of them from the blocks of any one segment, and exactly 4 from some segment.
All inputs are finite; a program needn't handle non-finite values.
Results may differ from the reference program's by a relative error of at most 0.0055.
Values may be sent and summed in bfloat16 or wider, within the bound.
A program may use at most 128 MiB of HBM per device.

```python
import math
import jax
import jax.numpy as jnp
from jax import lax

H = 16
HD = 128
BLK = 64
TOPK = 16
POOL = 32
TOK_DEV = 512
BLK_DEV = 8
TOKENS = 4096
NBLK = 64
CAP = 4
N_SEQ = 8


def query_key_pair(key):
    array_shape = (TOKENS, H * HD)
    key_field = jnp.clip(jax.random.normal(jax.random.fold_in(key, 31), array_shape, jnp.float32), -6.0, 6.0)
    query_field = jnp.clip(jax.random.normal(jax.random.fold_in(key, 32), array_shape, jnp.float32), -6.0, 6.0)
    return (query_field, key_field)


def draw_queries(key, part):
    return query_key_pair(key)[0].astype(jnp.bfloat16)


def draw_keys(key, part):
    return query_key_pair(key)[1].astype(jnp.bfloat16)


def draw_retrieved(key, part):
    writers = NBLK // BLK_DEV
    writer_heat = jax.random.randint(jax.random.fold_in(key, 21), (writers,), 0, 4)
    top_writer = jax.random.randint(jax.random.fold_in(key, 22), (), 0, writers)

    def one_segment(device_key):
        first_key, second_key, third_key, fourth_key = jax.random.split(device_key, 4)
        inner_pick = jax.vmap(lambda subkey: jax.random.permutation(subkey, BLK_DEV)[:CAP])(jax.random.split(first_key, writers))
        candidates = jnp.arange(writers, dtype=jnp.int32)[:, None] * BLK_DEV + inner_pick.astype(jnp.int32)
        int_noise = jax.random.randint(second_key, (writers, CAP), 0, 4)
        forced = (jnp.arange(writers, dtype=jnp.int32) == top_writer).astype(jnp.int32)[:, None] * 64
        tie_break = jax.random.permutation(third_key, writers * CAP).astype(jnp.int32).reshape(writers, CAP)
        pool_score = (int_noise + writer_heat[:, None] + forced) * (writers * CAP) + tie_break
        _, selected = lax.top_k(pool_score.reshape(-1), POOL)
        pool_blocks = candidates.reshape(-1)[selected]
        owner_row = jnp.arange(POOL, dtype=jnp.int32) % BLK_DEV
        row_ranks = jax.vmap(lambda subkey: jax.random.permutation(subkey, POOL))(jax.random.split(fourth_key, BLK_DEV)).astype(jnp.int32)
        owned = (owner_row[None, :] == jnp.arange(BLK_DEV, dtype=jnp.int32)[:, None]).astype(jnp.int32)
        _, chosen = lax.top_k(owned * POOL + row_ranks, TOPK)
        return pool_blocks[chosen]
    block_ids = jax.vmap(one_segment)(jax.random.split(key, writers))
    return block_ids.reshape(NBLK, TOPK).astype(jnp.int32)


def block_levels(key, shape, shards, least, largest):
    factor_of = 1.0
    for dim, blocks in shards:
        heights = jax.random.uniform(jax.random.fold_in(jax.random.fold_in(key, 6), dim), (blocks,), jnp.float32, least / len(shards), largest / len(shards))
        factor_of = factor_of * jnp.repeat(jnp.exp(heights), shape[dim] // blocks).reshape((-1,) + (1,) * (len(shape) - 1 - dim))
    return factor_of


def bell_draw(stream_key, extent, scale, bound, cuts=(), kind=jnp.bfloat16):
    loudness = block_levels(stream_key, extent, cuts, -0.22, 0.18) if cuts else 1.0
    values = jax.random.normal(stream_key, extent, jnp.float32) * scale * loudness
    return jnp.minimum(jnp.maximum(values, -bound), bound).astype(kind)


def setup_inputs(seed: int = 0) -> dict:
    seeds = jax.random.split(jax.random.key(seed), 7)
    return {
        "queries": draw_queries(jax.random.fold_in(seeds[6], 71), 0),
        "keys": draw_keys(jax.random.fold_in(seeds[6], 71), 0),
        "values": bell_draw(seeds[2], (TOKENS, H * HD), 1.0, 6.0, ((0, 8), (1, 4))),
        "grad_out": bell_draw(seeds[3], (TOKENS, H * HD), 1.0, 6.0, ((0, 8), (1, 4))),
        "retrieved": draw_retrieved(jax.random.fold_in(seeds[6], 71), 0),
        "mem_bias": jnp.clip(-2.0 + 3.0 * jax.random.uniform(seeds[5], (H,), jnp.float32) ** block_levels(seeds[5], (H,), ((0, 4),), -0.2, 0.2), -2.0, 1.0),
    }


def product(pattern, former, latter):
    return jnp.einsum(pattern, former.astype(jnp.float32), latter.astype(jnp.float32))

def attend_group(queries, grads, seg_keys, seg_values, mem_keys, mem_values, usable, bias, first_row):
    row_count, features = queries.shape
    head_count = bias.shape[0]
    head_size = features // head_count
    block_count, top_count, block_len, _ = mem_keys.shape
    seg_len = seg_keys.shape[0]
    score_scale = 1.0 / math.sqrt(head_size)
    query_heads = queries.reshape(block_count, block_len, head_count, head_size)
    grad_heads = grads.reshape(block_count, block_len, head_count, head_size)
    key_heads = seg_keys.reshape(seg_len, head_count, head_size)
    value_heads = seg_values.reshape(seg_len, head_count, head_size)
    mem_key_heads = mem_keys.reshape(block_count, top_count * block_len, head_count, head_size)
    mem_value_heads = mem_values.reshape(block_count, top_count * block_len, head_count, head_size)
    query_pos = first_row + jnp.arange(row_count, dtype=jnp.int32).reshape(block_count, 1, block_len, 1)
    key_pos = jnp.arange(seg_len, dtype=jnp.int32)
    local_ok = key_pos[None, None, None, :] <= query_pos
    memory_ok = jnp.broadcast_to(usable[:, :, None], (block_count, top_count, block_len)).reshape(block_count, 1, 1, top_count * block_len)
    local_score = product('nqhd,khd->nhqk', query_heads, key_heads) * score_scale
    local_score = jnp.where(local_ok, local_score, -1e+30)
    memory_score = product('nqhd,nkhd->nhqk', query_heads, mem_key_heads) * score_scale + bias[None, :, None, None]
    memory_score = jnp.where(memory_ok, memory_score, -1e+30)
    highest = jnp.maximum(lax.optimization_barrier(jnp.max(local_score, axis=-1, keepdims=True)), lax.optimization_barrier(jnp.max(memory_score, axis=-1, keepdims=True)))
    local_exp = jnp.exp(local_score - highest)
    memory_exp = jnp.exp(memory_score - highest)
    total_mass = lax.optimization_barrier(jnp.sum(local_exp, axis=-1, keepdims=True)) + lax.optimization_barrier(jnp.sum(memory_exp, axis=-1, keepdims=True))
    local_prob = local_exp / total_mass
    memory_prob = memory_exp / total_mass
    local_weight = local_prob.astype(jnp.bfloat16)
    memory_weight = memory_prob.astype(jnp.bfloat16)
    attended = product('nhqk,khd->nqhd', local_weight, value_heads) + product('nhqk,nkhd->nqhd', memory_weight, mem_value_heads)
    local_dprob = product('nqhd,khd->nhqk', grad_heads, value_heads)
    memory_dprob = product('nqhd,nkhd->nhqk', grad_heads, mem_value_heads)
    row_delta = lax.optimization_barrier(jnp.sum(local_prob * local_dprob, axis=-1, keepdims=True)) + lax.optimization_barrier(jnp.sum(memory_prob * memory_dprob, axis=-1, keepdims=True))
    local_dscore = (local_prob * (local_dprob - row_delta) * score_scale).astype(jnp.bfloat16)
    memory_dscore = (memory_prob * (memory_dprob - row_delta) * score_scale).astype(jnp.bfloat16)
    grad_query = product('nhqk,khd->nqhd', local_dscore, key_heads) + product('nhqk,nkhd->nqhd', memory_dscore, mem_key_heads)
    local_dkey = product('nhqk,nqhd->khd', local_dscore, query_heads).reshape(seg_len, features)
    local_dvalue = product('nhqk,nqhd->khd', local_weight, grad_heads).reshape(seg_len, features)
    memory_dkey = product('nhqk,nqhd->nkhd', memory_dscore, query_heads).reshape(block_count, top_count, block_len, features)
    memory_dvalue = product('nhqk,nqhd->nkhd', memory_weight, grad_heads).reshape(block_count, top_count, block_len, features)
    return (attended.reshape(row_count, features).astype(jnp.bfloat16), grad_query.reshape(row_count, features).astype(jnp.bfloat16), local_dkey, local_dvalue, memory_dkey, memory_dvalue)

def reference(queries, keys, values, grad_out, retrieved, mem_bias):
    features = H * HD
    group_rows = min(512, TOK_DEV)
    group_blocks = group_rows // BLK
    per_segment = TOK_DEV // group_rows
    key_blocks = keys.reshape(NBLK, BLK, features)
    value_blocks = values.reshape(NBLK, BLK, features)

    def group_step(inner_carry, group_index):
        seg_kgrad, seg_vgrad, mem_kgrad, mem_vgrad = inner_carry
        segment = group_index // per_segment
        first_row = group_index % per_segment * group_rows
        row_start = group_index * group_rows
        query_rows = lax.dynamic_slice_in_dim(queries, row_start, group_rows, 0)
        grad_rows = lax.dynamic_slice_in_dim(grad_out, row_start, group_rows, 0)
        seg_keys = lax.dynamic_slice_in_dim(keys, segment * TOK_DEV, TOK_DEV, 0)
        seg_values = lax.dynamic_slice_in_dim(values, segment * TOK_DEV, TOK_DEV, 0)
        named_blocks = lax.dynamic_slice_in_dim(retrieved, group_index * group_blocks, group_blocks, 0)
        block_index = group_index * group_blocks + jnp.arange(group_blocks, dtype=jnp.int32)
        usable = named_blocks < block_index[:, None]
        flat_named = named_blocks.reshape(-1)
        mem_keys = key_blocks[flat_named].reshape(group_blocks, TOPK, BLK, features)
        mem_values = value_blocks[flat_named].reshape(group_blocks, TOPK, BLK, features)
        results = attend_group(query_rows, grad_rows, seg_keys, seg_values, mem_keys, mem_values, usable, mem_bias, first_row)
        seg_kgrad = seg_kgrad + results[2]
        seg_vgrad = seg_vgrad + results[3]
        mem_kgrad = mem_kgrad.at[flat_named].add(results[4].reshape(group_blocks * TOPK, BLK, features))
        mem_vgrad = mem_vgrad.at[flat_named].add(results[5].reshape(group_blocks * TOPK, BLK, features))
        return ((seg_kgrad, seg_vgrad, mem_kgrad, mem_vgrad), (results[0], results[1]))

    def segment_step(state_carry, segment):
        key_grad, value_grad = state_carry
        zero_seg = jnp.zeros((TOK_DEV, features), jnp.float32)
        zero_mem = jnp.zeros((NBLK, BLK, features), jnp.float32)
        groups = segment * per_segment + jnp.arange(per_segment, dtype=jnp.int32)
        inner, outputs = lax.scan(group_step, (zero_seg, zero_seg, zero_mem, zero_mem), groups)
        rounded_keys = lax.optimization_barrier(inner[2].astype(jnp.bfloat16)).astype(jnp.float32)
        rounded_values = lax.optimization_barrier(inner[3].astype(jnp.bfloat16)).astype(jnp.float32)
        key_grad = key_grad + rounded_keys
        value_grad = value_grad + rounded_values
        seg_start = segment * BLK_DEV
        local_key = lax.dynamic_slice_in_dim(key_grad, seg_start, BLK_DEV, 0) + inner[0].reshape(BLK_DEV, BLK, features)
        local_value = lax.dynamic_slice_in_dim(value_grad, seg_start, BLK_DEV, 0) + inner[1].reshape(BLK_DEV, BLK, features)
        key_grad = lax.dynamic_update_slice_in_dim(key_grad, local_key, seg_start, 0)
        value_grad = lax.dynamic_update_slice_in_dim(value_grad, local_value, seg_start, 0)
        return ((key_grad, value_grad), outputs)
    zero_grads = jnp.zeros((NBLK, BLK, features), jnp.float32)
    finals, outputs = lax.scan(segment_step, (zero_grads, zero_grads), jnp.arange(N_SEQ, dtype=jnp.int32))
    attended = outputs[0].reshape(TOKENS, features)
    grad_queries = outputs[1].reshape(TOKENS, features)
    grad_keys = finals[0].reshape(TOKENS, features).astype(jnp.bfloat16)
    grad_values = finals[1].reshape(TOKENS, features).astype(jnp.bfloat16)
    return (attended, grad_queries, grad_keys, grad_values)
```

```python
import functools
import math

import jax
import jax.numpy as jnp
from jax import lax
from jax.experimental import pallas as pl
from jax.experimental.pallas import tpu as pltpu
from jax.sharding import PartitionSpec as P

BLK = 64
LOG2E = math.log2(math.e)
NEG = -1e30
MESH = pl.DeviceIdType.MESH
F32 = jnp.float32
BF16 = jnp.bfloat16


def matmul(left, right):
    return jnp.dot(left, right, preferred_element_type=F32)


def owner_core(segment):
    return lax.rem((segment + 1) // 2, 2)


def fused(
    dims,
    table_in,
    bias_ref,
    q_ref,
    k_ref,
    v_ref,
    g_ref,
    o_ref,
    dq_ref,
    dk_ref,
    dv_ref,
    table,
    q_buf,
    g_buf,
    k_buf,
    v_buf,
    kt_buf,
    vt_buf,
    dk_acc,
    dv_acc,
    part,
    stage,
    bias_rows,
    qt,
    gt,
    ot,
    dqt,
    stat,
    hop1_send,
    hop1_recv,
    hop2_send,
    hop2_recv,
    in_send,
    in_recv,
    fwd_send,
    fwd_recv,
    part_send,
    part_recv,
    out_send,
    out_recv,
):
    seq_count, head_dev, chips, seg_len, hd, rows_dev, top = dims
    seg_blocks = seg_len // BLK
    scale = 1.0 / math.sqrt(hd)
    me = lax.axis_index("seq")
    zed = lax.axis_index("head")
    chip = me // 2
    core = lax.rem(me, 2)
    sibling = chip * 2 + 1 - core

    barrier = pltpu.get_barrier_semaphore()
    for j in range(1, seq_count):
        pl.semaphore_signal(
            barrier, inc=1, device_id={"seq": lax.rem(me + j, seq_count)}, device_id_type=MESH
        )
    for j in range(1, head_dev):
        pl.semaphore_signal(
            barrier, inc=1, device_id={"head": lax.rem(zed + j, head_dev)}, device_id_type=MESH
        )
    pl.semaphore_wait(barrier, seq_count + head_dev - 2)

    def hop1(j):
        return pltpu.make_async_remote_copy(
            src_ref=table_in,
            dst_ref=table.at[me, zed],
            send_sem=hop1_send.at[j - 1],
            recv_sem=hop1_recv.at[j - 1],
            device_id={"head": lax.rem(zed + j, head_dev)},
            device_id_type=MESH,
        )

    for j in range(1, head_dev):
        hop1(j).start()
    table[me, zed] = table_in[...]

    arrays = ((k_ref, k_buf), (q_ref, q_buf), (v_ref, v_buf), (g_ref, g_buf))
    goes_to = owner_core(me)

    def push(a, j):
        src, buf = arrays[a]
        target_chip = lax.rem(chip + 1 + j, chips)
        columns = pl.ds(pl.multiple_of(target_chip * hd, hd), hd)
        slot = me if a in (0, 2) else chip
        return (
            src.at[:, columns],
            buf.at[slot],
            target_chip * 2 + goes_to,
            in_send.at[a, j],
            in_recv.at[a, chip],
        )

    def push_remote(a, j):
        src, dst, device, send, recv = push(a, j)
        return pltpu.make_async_remote_copy(
            src_ref=src,
            dst_ref=dst,
            send_sem=send,
            recv_sem=recv,
            device_id={"seq": device},
            device_id_type=MESH,
        )

    for a in range(4):
        for j in range(chips - 1):
            push_remote(a, j).start()

        @pl.when(goes_to != core)
        def _():
            push_remote(a, chips - 1).start()

        @pl.when(goes_to == core)
        def _():
            src, dst, _, _, recv = push(a, chips - 1)
            pltpu.make_async_copy(src, dst, recv).start()

    for j in range(1, head_dev):
        hop1(j).wait()

    def hop2(j):
        return pltpu.make_async_remote_copy(
            src_ref=table.at[me],
            dst_ref=table.at[me],
            send_sem=hop2_send.at[j - 1],
            recv_sem=hop2_recv.at[j - 1],
            device_id={"seq": lax.rem(me + j, seq_count)},
            device_id_type=MESH,
        )

    for j in range(1, seq_count):
        hop2(j).start()

    dk_acc[...] = jnp.zeros_like(dk_acc)
    dv_acc[...] = jnp.zeros_like(dv_acc)

    def segment_of(pair, which):
        return pair * 2 + lax.rem(pair + which, 2)

    def in_wait(a, pair):
        _, buf = arrays[a]
        slot = segment_of(pair, core) if a in (0, 2) else pair
        pltpu.make_async_copy(buf.at[slot], buf.at[slot], in_recv.at[a, pair]).wait()

    def forward(a, pair, which):
        buf = k_buf if a == 0 else v_buf
        spot = buf.at[segment_of(pair, which)]
        return pltpu.make_async_remote_copy(
            src_ref=spot,
            dst_ref=spot,
            send_sem=fwd_send.at[a, pair],
            recv_sem=fwd_recv.at[a, pair],
            device_id={"seq": sibling},
            device_id_type=MESH,
        )

    for kind in range(2):
        for pair in range(chips):
            in_wait(2 * kind, pair)
            forward(kind, pair, core).start()
            in_wait(2 * kind + 1, pair)
    for j in range(1, seq_count):
        hop2(j).wait()
    for pair in range(chips):
        for kind, buf, turned in ((0, k_buf, kt_buf), (1, v_buf, vt_buf)):
            mine = segment_of(pair, core)
            turned[mine] = buf[mine].T
            forward(kind, pair, 1 - core).wait_recv()
            other = segment_of(pair, 1 - core)
            turned[other] = buf[other].T
            forward(kind, pair, core).wait_send()

    bias2 = bias_ref[0, chip]
    both2 = bias_ref[1, chip]
    score2 = scale * LOG2E
    kb_seg = (seg_blocks, 1, seg_len)
    tile = (seg_blocks, BLK, seg_len)

    def scores(k, rows):
        raw = matmul(k_buf[k], qt[...]).reshape(tile)
        return raw * score2 + rows.reshape(kb_seg)

    def triangle(value):
        key = lax.broadcasted_iota(jnp.int32, (seg_len, seg_len), 0)
        query = lax.broadcasted_iota(jnp.int32, (seg_len, seg_len), 1)
        return jnp.where((key <= query).reshape(tile), value, NEG)

    def rows_of(k):
        return bias_rows[pl.ds(pl.multiple_of(k * seg_blocks, seg_blocks), seg_blocks), :]

    def out_send_copy(a, pair, seg):
        ref = (o_ref, dq_ref, dk_ref, dv_ref)[a]
        return pltpu.make_async_remote_copy(
            src_ref=stage.at[a, pair],
            dst_ref=ref.at[:, pl.ds(pl.multiple_of(chip * hd, hd), hd)],
            send_sem=out_send.at[a, pair],
            recv_sem=out_recv.at[a, chip],
            device_id={"seq": seg},
            device_id_type=MESH,
        )

    def emit(a, pair, seg):
        @pl.when(seg != me)
        def _():
            out_send_copy(a, pair, seg).start()

        @pl.when(seg == me)
        def _():
            ref = (o_ref, dq_ref, dk_ref, dv_ref)[a]
            pltpu.make_async_copy(
                stage.at[a, pair],
                ref.at[:, pl.ds(pl.multiple_of(chip * hd, hd), hd)],
                out_recv.at[a, chip],
            ).start()

    def part_copy(kind, pair, which):
        acc = dk_acc if kind == 0 else dv_acc
        return pltpu.make_async_remote_copy(
            src_ref=acc.at[segment_of(pair, which)],
            dst_ref=part.at[kind, pair],
            send_sem=part_send.at[kind, pair],
            recv_sem=part_recv.at[kind, pair],
            device_id={"seq": sibling},
            device_id_type=MESH,
        )

    def each_segment(step, carry):
        pair = chips - 1 - step
        seg = segment_of(pair, core)
        lists = table[seg].reshape(head_dev * 8, 128).astype(BF16)
        slot = lax.broadcasted_iota(jnp.int32, (head_dev * 8, seg_len), 0)
        lane_block = lax.broadcasted_iota(jnp.int32, (head_dev * 8, seg_len), 1) // BLK
        at_block = (slot // 8) * rows_dev + lax.rem(slot, 8)
        pick = jnp.where((lax.rem(slot, 8) < rows_dev) & (at_block == lane_block), 1.0, 0.0)
        named_of = lax.dot_general(
            lists, pick.astype(BF16), (((0,), (0,)), ((), ())), preferred_element_type=F32
        )
        kb = lax.broadcasted_iota(jnp.int32, (seq_count * seg_blocks, seg_len), 0)
        block = (
            seg * seg_blocks
            + lax.broadcasted_iota(jnp.int32, (seq_count * seg_blocks, seg_len), 1) // BLK
        )
        kb_f = kb.astype(F32)
        named = named_of[0:1, :] == kb_f
        for t in range(1, top):
            named = named | (named_of[t : t + 1, :] == kb_f)
        same = kb >= seg * seg_blocks
        before = jnp.where(
            same, jnp.where(named, both2, 0.0), jnp.where(named, bias2, NEG)
        )
        bias_rows[...] = jnp.where(kb < block, before, jnp.where(kb == block, 0.0, NEG))

        qt[...] = q_buf[pair].T
        gt[...] = g_buf[pair].T

        first = triangle(scores(seg, rows_of(seg)))
        top_row = jnp.max(jnp.max(first, axis=0), axis=0, keepdims=True)
        weight = jnp.exp2(first - top_row.reshape(1, 1, seg_len))
        stat[0:1, :] = top_row
        stat[1:2, :] = jnp.sum(jnp.sum(weight, axis=0), axis=0, keepdims=True)
        ot[...] = matmul(vt_buf[seg], weight.reshape(seg_len, seg_len).astype(BF16))

        def forward_tile(k, c):
            value = scores(k, rows_of(k))
            old = stat[0:1, :]
            new = jnp.maximum(old, jnp.max(jnp.max(value, axis=0), axis=0, keepdims=True))
            shrink = jnp.exp2(old - new)
            weight = jnp.exp2(value - new.reshape(1, 1, seg_len))
            stat[0:1, :] = new
            stat[1:2, :] = stat[1:2, :] * shrink + jnp.sum(
                jnp.sum(weight, axis=0), axis=0, keepdims=True
            )
            ot[...] = ot[...] * shrink + matmul(
                vt_buf[k], weight.reshape(seg_len, seg_len).astype(BF16)
            )
            return c

        lax.fori_loop(0, seg, forward_tile, 0)
        mass = stat[1:2, :]
        ot[...] = ot[...] / mass
        stage[0, pair] = ot[...].T.astype(BF16)
        emit(0, pair, seg)
        lse = stat[0:1, :] + jnp.log2(mass)
        stat[2:3, :] = jnp.sum(ot[...] * gt[...].astype(F32), axis=0, keepdims=True)
        stat[3:4, :] = lse
        dqt[...] = jnp.zeros_like(dqt)

        def backward_tile(k, diagonal):
            value = scores(k, rows_of(k) - stat[3:4, :])
            if diagonal:
                value = triangle(value)
            prob = jnp.exp2(value).reshape(seg_len, seg_len)
            dprob = matmul(v_buf[k], gt[...])
            dscore = (prob * (dprob - stat[2:3, :])).astype(BF16)
            dv_acc[k] += matmul(prob.astype(BF16), g_buf[pair])
            dk_acc[k] += matmul(dscore, q_buf[pair])
            dqt[...] += matmul(kt_buf[k], dscore)

        backward_tile(seg, True)

        def backward_step(k, c):
            backward_tile(k, False)
            return c

        lax.fori_loop(0, seg, backward_step, 0)
        part_copy(0, pair, 1 - core).start()
        part_copy(1, pair, 1 - core).start()
        stage[1, pair] = (dqt[...] * scale).T.astype(BF16)
        emit(1, pair, seg)
        part_copy(0, pair, 1 - core).wait_recv()
        stage[2, pair] = ((dk_acc[seg] + part[0, pair]) * scale).astype(BF16)
        emit(2, pair, seg)
        part_copy(1, pair, 1 - core).wait_recv()
        stage[3, pair] = (dv_acc[seg] + part[1, pair]).astype(BF16)
        emit(3, pair, seg)
        return carry

    lax.fori_loop(0, chips, each_segment, 0)

    for a in range(4):
        ref = (o_ref, dq_ref, dk_ref, dv_ref)[a]
        for j in range(chips - 1):
            push_remote(a, j).wait_send()

        @pl.when(goes_to != core)
        def _():
            push_remote(a, chips - 1).wait_send()

        for pair in range(chips):
            seg = segment_of(pair, core)

            @pl.when(seg != me)
            def _():
                out_send_copy(a, pair, seg).wait_send()

            if a < 2:
                part_copy(a, pair, 1 - core).wait_send()
            spot = ref.at[:, pl.ds(pair * hd, hd)]
            pltpu.make_async_copy(spot, spot, out_recv.at[a, pair]).wait()


def by_heads(queries, keys, values, grad_out, retrieved, mem_bias):
    seq_count = lax.axis_size("seq")
    head_dev = lax.axis_size("head")
    seg_len, features = keys.shape
    heads = mem_bias.shape[0]
    hd = features // heads
    chips = seq_count // 2
    rows_dev, top = retrieved.shape
    seg_blocks = seg_len // BLK
    table = jnp.pad(retrieved.astype(F32), ((0, 8 - rows_dev), (0, 128 - top)))
    bias = jnp.stack([mem_bias * LOG2E, jnp.log1p(jnp.exp(mem_bias)) * LOG2E])
    dims = (seq_count, head_dev, chips, seg_len, hd, rows_dev, top)
    dma = pltpu.SemaphoreType.DMA
    vm = pltpu.VMEM
    anywhere = pl.BlockSpec(memory_space=pl.ANY)
    out = jax.ShapeDtypeStruct((seg_len, features), BF16)
    return pl.pallas_call(
        functools.partial(fused, dims),
        out_shape=(out,) * 4,
        in_specs=[
            pl.BlockSpec(memory_space=pltpu.VMEM),
            pl.BlockSpec(memory_space=pltpu.SMEM),
        ]
        + [anywhere] * 4,
        out_specs=(anywhere,) * 4,
        scratch_shapes=[
            vm((seq_count, head_dev, 8, 128), F32),
            vm((chips, seg_len, hd), BF16),
            vm((chips, seg_len, hd), BF16),
            vm((seq_count, seg_len, hd), BF16),
            vm((seq_count, seg_len, hd), BF16),
            vm((seq_count, hd, seg_len), BF16),
            vm((seq_count, hd, seg_len), BF16),
            vm((seq_count, seg_len, hd), F32),
            vm((seq_count, seg_len, hd), F32),
            vm((2, chips, seg_len, hd), F32),
            vm((4, chips, seg_len, hd), BF16),
            vm((seq_count * seg_blocks, seg_len), F32),
            vm((hd, seg_len), BF16),
            vm((hd, seg_len), BF16),
            vm((hd, seg_len), F32),
            vm((hd, seg_len), F32),
            vm((8, seg_len), F32),
            dma((head_dev - 1,)),
            dma((head_dev - 1,)),
            dma((seq_count - 1,)),
            dma((seq_count - 1,)),
            dma((4, chips)),
            dma((4, chips)),
            dma((2, chips)),
            dma((2, chips)),
            dma((2, chips)),
            dma((2, chips)),
            dma((4, chips)),
            dma((4, chips)),
        ],
        compiler_params=pltpu.CompilerParams(
            collective_id=0, has_side_effects=True, vmem_limit_bytes=56 * 1024 * 1024
        ),
    )(table, bias, queries, keys, values, grad_out)


def by_segments(queries, keys, values, grad_out, retrieved, mem_bias):
    seq_count = lax.axis_size("seq")
    position = lax.axis_index("seq")
    seg_len, features = keys.shape
    heads = mem_bias.shape[0]
    hd = features // heads
    seg_blocks = seg_len // BLK
    scale = 1.0 / math.sqrt(hd)
    lists = lax.all_gather(retrieved, "head", axis=0, tiled=True)
    all_keys = lax.all_gather(keys, "seq").reshape(seq_count, seg_len, heads, hd)
    all_values = lax.all_gather(values, "seq").reshape(seq_count, seg_len, heads, hd)
    q = queries.reshape(seg_len, heads, hd)
    g = grad_out.reshape(seg_len, heads, hd)
    row = jnp.arange(seg_len, dtype=jnp.int32)

    def score(k, key_seg):
        kb = k * seg_blocks + jnp.arange(seg_blocks, dtype=jnp.int32)
        block = position * seg_blocks + jnp.arange(seg_blocks, dtype=jnp.int32)
        named = jnp.any(lists[:, :, None] == kb[None, None, :], axis=1)
        named = named & (kb[None, :] < block[:, None])
        named = jnp.repeat(jnp.repeat(named, BLK, axis=0), BLK, axis=1)
        local = (k == position) & (row[None, :] <= row[:, None])
        bias = mem_bias[:, None, None]
        extra = jnp.where(
            local[None],
            jnp.where(named[None], jnp.log1p(jnp.exp(bias)), 0.0),
            jnp.where(named[None], bias, NEG),
        )
        return jnp.einsum("qhd,khd->hqk", q, key_seg, preferred_element_type=F32) * scale + extra

    def forward(carry, k):
        best, mass, acc = carry
        value = score(k, all_keys[k])
        new = jnp.maximum(best, jnp.max(value, axis=-1, keepdims=True))
        shrink = jnp.exp(best - new)
        weight = jnp.where(value > 0.5 * NEG, jnp.exp(value - new), 0.0)
        acc = acc * shrink + jnp.einsum(
            "hqk,khd->hqd", weight.astype(BF16), all_values[k], preferred_element_type=F32
        )
        return (new, mass * shrink + jnp.sum(weight, axis=-1, keepdims=True), acc), None

    start = (
        jnp.full((heads, seg_len, 1), NEG, F32),
        jnp.zeros((heads, seg_len, 1), F32),
        jnp.zeros((heads, seg_len, hd), F32),
    )
    order = jnp.arange(seq_count, dtype=jnp.int32)
    (best, mass, acc), _ = lax.scan(forward, start, order)
    attended = acc / mass
    lse = best + jnp.log(mass)
    delta = jnp.sum(attended * g.astype(F32).transpose(1, 0, 2), axis=-1, keepdims=True)

    def backward(dq, k):
        prob = jnp.exp(score(k, all_keys[k]) - lse)
        dprob = jnp.einsum("qhd,khd->hqk", g, all_values[k], preferred_element_type=F32)
        dscore = (prob * (dprob - delta) * scale).astype(BF16)
        dq = dq + jnp.einsum("hqk,khd->hqd", dscore, all_keys[k], preferred_element_type=F32)
        dk = jnp.einsum("hqk,qhd->khd", dscore, q, preferred_element_type=F32)
        dv = jnp.einsum("hqk,qhd->khd", prob.astype(BF16), g, preferred_element_type=F32)
        return dq, (dk.reshape(seg_len, features), dv.reshape(seg_len, features))

    dq, (dk, dv) = lax.scan(backward, jnp.zeros((heads, seg_len, hd), F32), order)
    dk = lax.psum_scatter(dk, "seq", scatter_dimension=0)
    dv = lax.psum_scatter(dv, "seq", scatter_dimension=0)

    def rows(x):
        return x.transpose(1, 0, 2).reshape(seg_len, features).astype(BF16)

    return rows(attended), rows(dq), dk.astype(BF16), dv.astype(BF16)


def shards(queries, keys, values, grad_out, retrieved, mem_bias):
    heads = mem_bias.shape[0]
    hd = keys.shape[1] // heads
    if (
        lax.axis_size("seq") == 2 * heads
        and hd % 128 == 0
        and retrieved.shape[0] <= 8
        and heads > 1
        and lax.axis_size("head") > 1
    ):
        return by_heads(queries, keys, values, grad_out, retrieved, mem_bias)
    return by_segments(queries, keys, values, grad_out, retrieved, mem_bias)


def solution(mesh):
    placed = (
        P("seq", "head"),
        P("seq", "head"),
        P("seq", "head"),
        P("seq", "head"),
        P(("seq", "head"), None),
        P("head"),
    )
    return jax.shard_map(
        shards,
        mesh=mesh,
        in_specs=placed,
        out_specs=(P("seq", "head"), P("seq", "head"), P("seq", "head"), P("seq", "head")),
        check_vma=False,
    )
```

```python
import functools
import math

import jax
import jax.numpy as jnp
from jax import lax
from jax.experimental import pallas as pl
from jax.experimental.pallas import tpu as pltpu
from jax.sharding import PartitionSpec as P

BLK = 64
LOG2E = math.log2(math.e)
NEG = -1e30
MESH = pl.DeviceIdType.MESH
F32 = jnp.float32
BF16 = jnp.bfloat16


def matmul(left, right):
    return jnp.dot(left, right, preferred_element_type=F32)


def owner_core(segment):
    return lax.rem((segment + 1) // 2, 2)


def fused(
    dims,
    table_in,
    bias_ref,
    q_ref,
    k_ref,
    v_ref,
    g_ref,
    o_ref,
    dq_ref,
    dk_ref,
    dv_ref,
    table,
    q_buf,
    g_buf,
    k_buf,
    v_buf,
    kt_buf,
    vt_buf,
    dk_acc,
    dv_acc,
    part,
    stage,
    bias_rows,
    qt,
    gt,
    ot,
    dqt,
    stat,
    hop1_send,
    hop1_recv,
    hop2_send,
    hop2_recv,
    in_send,
    in_recv,
    fwd_send,
    fwd_recv,
    part_send,
    part_recv,
    out_send,
    out_recv,
):
    seq_count, head_dev, chips, seg_len, hd, rows_dev, top = dims
    seg_blocks = seg_len // BLK
    scale = 1.0 / math.sqrt(hd)
    me = lax.axis_index("seq")
    zed = lax.axis_index("head")
    chip = me // 2
    core = lax.rem(me, 2)
    sibling = chip * 2 + 1 - core

    table[me, zed] = jnp.zeros((8, 128), F32)
    table[me, zed, 0:rows_dev, 0:top] = table_in[...].astype(F32)

    barrier = pltpu.get_barrier_semaphore()
    for j in range(1, seq_count):
        pl.semaphore_signal(
            barrier, inc=1, device_id={"seq": lax.rem(me + j, seq_count)}, device_id_type=MESH
        )
    for j in range(1, head_dev):
        pl.semaphore_signal(
            barrier, inc=1, device_id={"head": lax.rem(zed + j, head_dev)}, device_id_type=MESH
        )
    pl.semaphore_wait(barrier, seq_count + head_dev - 2)

    def hop1(j):
        return pltpu.make_async_remote_copy(
            src_ref=table.at[me, zed],
            dst_ref=table.at[me, zed],
            send_sem=hop1_send.at[j - 1],
            recv_sem=hop1_recv.at[j - 1],
            device_id={"head": lax.rem(zed + j, head_dev)},
            device_id_type=MESH,
        )

    for j in range(1, head_dev):
        hop1(j).start()

    arrays = ((k_ref, k_buf), (q_ref, q_buf), (v_ref, v_buf), (g_ref, g_buf))
    goes_to = owner_core(me)

    def push(a, j):
        src, buf = arrays[a]
        target_chip = lax.rem(chip + 1 + j, chips)
        columns = pl.ds(pl.multiple_of(target_chip * hd, hd), hd)
        slot = me if a in (0, 2) else chip
        return (
            src.at[:, columns],
            buf.at[slot],
            target_chip * 2 + goes_to,
            in_send.at[a, j],
            in_recv.at[a, chip],
        )

    def push_remote(a, j):
        src, dst, device, send, recv = push(a, j)
        return pltpu.make_async_remote_copy(
            src_ref=src,
            dst_ref=dst,
            send_sem=send,
            recv_sem=recv,
            device_id={"seq": device},
            device_id_type=MESH,
        )

    for a in range(4):
        for j in range(chips - 1):
            push_remote(a, j).start()

        @pl.when(goes_to != core)
        def _():
            push_remote(a, chips - 1).start()

        @pl.when(goes_to == core)
        def _():
            src, dst, _, _, recv = push(a, chips - 1)
            pltpu.make_async_copy(src, dst, recv).start()

    for j in range(1, head_dev):
        hop1(j).wait()

    def hop2(j):
        return pltpu.make_async_remote_copy(
            src_ref=table.at[me],
            dst_ref=table.at[me],
            send_sem=hop2_send.at[j - 1],
            recv_sem=hop2_recv.at[j - 1],
            device_id={"seq": lax.rem(me + j, seq_count)},
            device_id_type=MESH,
        )

    for j in range(1, seq_count):
        hop2(j).start()

    dk_acc[...] = jnp.zeros_like(dk_acc)
    dv_acc[...] = jnp.zeros_like(dv_acc)
    dqt[...] = jnp.zeros_like(dqt)

    def segment_of(pair, which):
        return pair * 2 + lax.rem(pair + which, 2)

    def in_wait(a, pair):
        _, buf = arrays[a]
        slot = segment_of(pair, core) if a in (0, 2) else pair
        pltpu.make_async_copy(buf.at[slot], buf.at[slot], in_recv.at[a, pair]).wait()

    def forward(a, pair, which):
        buf = k_buf if a == 0 else v_buf
        spot = buf.at[segment_of(pair, which)]
        return pltpu.make_async_remote_copy(
            src_ref=spot,
            dst_ref=spot,
            send_sem=fwd_send.at[a, pair],
            recv_sem=fwd_recv.at[a, pair],
            device_id={"seq": sibling},
            device_id_type=MESH,
        )

    for kind in range(2):
        for pair in range(chips):
            in_wait(2 * kind, pair)
            forward(kind, pair, core).start()
            if kind == 0:
                in_wait(1, pair)
    for j in range(1, seq_count):
        hop2(j).wait()
    for pair in range(chips):
        for kind, buf, turned in ((0, k_buf, kt_buf), (1, v_buf, vt_buf)):
            mine = segment_of(pair, core)
            turned[mine] = buf[mine].T
            forward(kind, pair, 1 - core).wait_recv()
            other = segment_of(pair, 1 - core)
            turned[other] = buf[other].T
            forward(kind, pair, core).wait_send()

    bias_row = jnp.full((1, seg_len), bias_ref[0, chip], F32)
    bias2 = bias_row * LOG2E
    both2 = jnp.log(1.0 + jnp.exp(bias_row)) * LOG2E
    score2 = scale * LOG2E
    kb_seg = (seg_blocks, 1, seg_len)
    tile = (seg_blocks, BLK, seg_len)

    def scores(k, rows, pair):
        raw = matmul(k_buf[k], qt[pair]).reshape(tile)
        return raw * score2 + rows.reshape(kb_seg)

    def triangle(value):
        key = lax.broadcasted_iota(jnp.int32, (seg_len, seg_len), 0)
        query = lax.broadcasted_iota(jnp.int32, (seg_len, seg_len), 1)
        return jnp.where((key <= query).reshape(tile), value, NEG)

    def rows_of(k, pair):
        return bias_rows[pair, pl.ds(pl.multiple_of(k * seg_blocks, seg_blocks), seg_blocks), :]

    def out_send_copy(a, pair, seg):
        ref = (o_ref, dq_ref, dk_ref, dv_ref)[a]
        return pltpu.make_async_remote_copy(
            src_ref=stage.at[a, pair],
            dst_ref=ref.at[:, pl.ds(pl.multiple_of(chip * hd, hd), hd)],
            send_sem=out_send.at[a, pair],
            recv_sem=out_recv.at[a, chip],
            device_id={"seq": seg},
            device_id_type=MESH,
        )

    def emit(a, pair, seg):
        @pl.when(seg != me)
        def _():
            out_send_copy(a, pair, seg).start()

        @pl.when(seg == me)
        def _():
            ref = (o_ref, dq_ref, dk_ref, dv_ref)[a]
            pltpu.make_async_copy(
                stage.at[a, pair],
                ref.at[:, pl.ds(pl.multiple_of(chip * hd, hd), hd)],
                out_recv.at[a, chip],
            ).start()

    def part_copy(kind, pair, which):
        acc = dk_acc if kind == 0 else dv_acc
        return pltpu.make_async_remote_copy(
            src_ref=acc.at[segment_of(pair, which)],
            dst_ref=part.at[kind, pair],
            send_sem=part_send.at[kind, pair],
            recv_sem=part_recv.at[kind, pair],
            device_id={"seq": sibling},
            device_id_type=MESH,
        )

    def turn(step):
        return lax.rem(chip + 1 + step, chips)

    def forward_segment(step, carry):
        pair = turn(step)
        seg = segment_of(pair, core)
        lists = table[seg].reshape(head_dev * 8, 128).astype(BF16)
        slot = lax.broadcasted_iota(jnp.int32, (head_dev * 8, seg_len), 0)
        lane_block = lax.broadcasted_iota(jnp.int32, (head_dev * 8, seg_len), 1) // BLK
        at_block = (slot // 8) * rows_dev + lax.rem(slot, 8)
        pick = jnp.where((lax.rem(slot, 8) < rows_dev) & (at_block == lane_block), 1.0, 0.0)
        named_of = lax.dot_general(
            lists, pick.astype(BF16), (((0,), (0,)), ((), ())), preferred_element_type=F32
        )
        kb = lax.broadcasted_iota(jnp.int32, (seq_count * seg_blocks, seg_len), 0)
        block = (
            seg * seg_blocks
            + lax.broadcasted_iota(jnp.int32, (seq_count * seg_blocks, seg_len), 1) // BLK
        )
        kb_f = kb.astype(F32)
        named = named_of[0:1, :] == kb_f
        for t in range(1, top):
            named = named | (named_of[t : t + 1, :] == kb_f)
        same = kb >= seg * seg_blocks
        before = jnp.where(
            same, jnp.where(named, both2, 0.0), jnp.where(named, bias2, NEG)
        )
        bias_rows[pair] = jnp.where(kb < block, before, jnp.where(kb == block, 0.0, NEG))

        qt[pair] = q_buf[pair].T

        first = triangle(scores(seg, rows_of(seg, pair), pair))
        top_row = jnp.max(jnp.max(first, axis=0), axis=0, keepdims=True)
        weight = jnp.exp2(first - top_row.reshape(1, 1, seg_len))
        stat[pair, 0:1, :] = top_row
        stat[pair, 1:2, :] = jnp.sum(jnp.sum(weight, axis=0), axis=0, keepdims=True)
        ot[pair] = matmul(vt_buf[seg], weight.reshape(seg_len, seg_len).astype(BF16))

        def forward_tile(k, c):
            value = scores(k, rows_of(k, pair), pair)
            old = stat[pair, 0:1, :]
            new = jnp.maximum(old, jnp.max(jnp.max(value, axis=0), axis=0, keepdims=True))
            shrink = jnp.exp2(old - new)
            weight = jnp.exp2(value - new.reshape(1, 1, seg_len))
            stat[pair, 0:1, :] = new
            stat[pair, 1:2, :] = stat[pair, 1:2, :] * shrink + jnp.sum(
                jnp.sum(weight, axis=0), axis=0, keepdims=True
            )
            ot[pair] = ot[pair] * shrink + matmul(
                vt_buf[k], weight.reshape(seg_len, seg_len).astype(BF16)
            )
            return c

        lax.fori_loop(0, seg, forward_tile, 0)
        mass = stat[pair, 1:2, :]
        ot[pair] = ot[pair] / mass
        stage[0, pair] = ot[pair].T.astype(BF16)
        emit(0, pair, seg)
        stat[pair, 3:4, :] = stat[pair, 0:1, :] + jnp.log2(mass)
        return carry

    lax.fori_loop(0, chips, forward_segment, 0)

    for pair in range(chips):
        in_wait(3, pair)
        gt[pair] = g_buf[pair].T
        stat[pair, 2:3, :] = jnp.sum(ot[pair] * gt[pair].astype(F32), axis=0, keepdims=True)

    def backward_tile(k, pair, diagonal):
        value = scores(k, rows_of(k, pair) - stat[pair, 3:4, :], pair)
        if diagonal:
            value = triangle(value)
        prob = jnp.exp2(value).reshape(seg_len, seg_len)
        dprob = matmul(v_buf[k], gt[pair])
        dscore = (prob * (dprob - stat[pair, 2:3, :])).astype(BF16)
        dv_acc[k] += matmul(prob.astype(BF16), g_buf[pair])
        dk_acc[k] += matmul(dscore, q_buf[pair])
        dqt[pair] += matmul(kt_buf[k], dscore)

    def finish_pair(step, carry):
        pair = turn(step)
        seg = segment_of(pair, core)

        def visit(index, c):
            other = index // 2
            query_pair = jnp.maximum(pair, other)
            k = jnp.minimum(pair, other) * 2 + lax.rem(index, 2)
            query_seg = segment_of(query_pair, core)
            live = lax.rem(other - chip - 1 + chips, chips) >= step

            @pl.when(live & (k < query_seg))
            def _():
                backward_tile(k, query_pair, False)

            @pl.when(live & (k == query_seg))
            def _():
                backward_tile(k, query_pair, True)

            return c

        lax.fori_loop(0, 2 * chips, visit, 0)
        part_copy(0, pair, 1 - core).start()
        part_copy(1, pair, 1 - core).start()
        stage[1, pair] = (dqt[pair] * scale).T.astype(BF16)
        emit(1, pair, seg)
        part_copy(0, pair, 1 - core).wait_recv()
        stage[2, pair] = ((dk_acc[seg] + part[0, pair]) * scale).astype(BF16)
        emit(2, pair, seg)
        part_copy(1, pair, 1 - core).wait_recv()
        stage[3, pair] = (dv_acc[seg] + part[1, pair]).astype(BF16)
        emit(3, pair, seg)
        return carry

    lax.fori_loop(0, chips, finish_pair, 0)

    for a in range(4):
        ref = (o_ref, dq_ref, dk_ref, dv_ref)[a]
        for j in range(chips - 1):
            push_remote(a, j).wait_send()

        @pl.when(goes_to != core)
        def _():
            push_remote(a, chips - 1).wait_send()

        for pair in range(chips):
            seg = segment_of(pair, core)

            @pl.when(seg != me)
            def _():
                out_send_copy(a, pair, seg).wait_send()

            if a < 2:
                part_copy(a, pair, 1 - core).wait_send()
            spot = ref.at[:, pl.ds(pair * hd, hd)]
            pltpu.make_async_copy(spot, spot, out_recv.at[a, pair]).wait()


def by_heads(queries, keys, values, grad_out, retrieved, mem_bias):
    seq_count = lax.axis_size("seq")
    head_dev = lax.axis_size("head")
    seg_len, features = keys.shape
    heads = mem_bias.shape[0]
    hd = features // heads
    chips = seq_count // 2
    rows_dev, top = retrieved.shape
    seg_blocks = seg_len // BLK
    dims = (seq_count, head_dev, chips, seg_len, hd, rows_dev, top)
    dma = pltpu.SemaphoreType.DMA
    vm = pltpu.VMEM
    anywhere = pl.BlockSpec(memory_space=pl.ANY)
    out = jax.ShapeDtypeStruct((seg_len, features), BF16)
    return pl.pallas_call(
        functools.partial(fused, dims),
        out_shape=(out,) * 4,
        in_specs=[
            pl.BlockSpec(memory_space=pltpu.VMEM),
            pl.BlockSpec(memory_space=pltpu.SMEM),
        ]
        + [anywhere] * 4,
        out_specs=(anywhere,) * 4,
        scratch_shapes=[
            vm((seq_count, head_dev, 8, 128), F32),
            vm((chips, seg_len, hd), BF16),
            vm((chips, seg_len, hd), BF16),
            vm((seq_count, seg_len, hd), BF16),
            vm((seq_count, seg_len, hd), BF16),
            vm((seq_count, hd, seg_len), BF16),
            vm((seq_count, hd, seg_len), BF16),
            vm((seq_count, seg_len, hd), F32),
            vm((seq_count, seg_len, hd), F32),
            vm((2, chips, seg_len, hd), F32),
            vm((4, chips, seg_len, hd), BF16),
            vm((chips, seq_count * seg_blocks, seg_len), F32),
            vm((chips, hd, seg_len), BF16),
            vm((chips, hd, seg_len), BF16),
            vm((chips, hd, seg_len), F32),
            vm((chips, hd, seg_len), F32),
            vm((chips, 8, seg_len), F32),
            dma((head_dev - 1,)),
            dma((head_dev - 1,)),
            dma((seq_count - 1,)),
            dma((seq_count - 1,)),
            dma((4, chips)),
            dma((4, chips)),
            dma((2, chips)),
            dma((2, chips)),
            dma((2, chips)),
            dma((2, chips)),
            dma((4, chips)),
            dma((4, chips)),
        ],
        compiler_params=pltpu.CompilerParams(
            collective_id=0, has_side_effects=True, vmem_limit_bytes=56 * 1024 * 1024
        ),
    )(retrieved, mem_bias.reshape(1, heads), queries, keys, values, grad_out)


def by_segments(queries, keys, values, grad_out, retrieved, mem_bias):
    seq_count = lax.axis_size("seq")
    position = lax.axis_index("seq")
    seg_len, features = keys.shape
    heads = mem_bias.shape[0]
    hd = features // heads
    seg_blocks = seg_len // BLK
    scale = 1.0 / math.sqrt(hd)
    lists = lax.all_gather(retrieved, "head", axis=0, tiled=True)
    all_keys = lax.all_gather(keys, "seq").reshape(seq_count, seg_len, heads, hd)
    all_values = lax.all_gather(values, "seq").reshape(seq_count, seg_len, heads, hd)
    q = queries.reshape(seg_len, heads, hd)
    g = grad_out.reshape(seg_len, heads, hd)
    row = jnp.arange(seg_len, dtype=jnp.int32)

    def score(k, key_seg):
        kb = k * seg_blocks + jnp.arange(seg_blocks, dtype=jnp.int32)
        block = position * seg_blocks + jnp.arange(seg_blocks, dtype=jnp.int32)
        named = jnp.any(lists[:, :, None] == kb[None, None, :], axis=1)
        named = named & (kb[None, :] < block[:, None])
        named = jnp.repeat(jnp.repeat(named, BLK, axis=0), BLK, axis=1)
        local = (k == position) & (row[None, :] <= row[:, None])
        bias = mem_bias[:, None, None]
        extra = jnp.where(
            local[None],
            jnp.where(named[None], jnp.log1p(jnp.exp(bias)), 0.0),
            jnp.where(named[None], bias, NEG),
        )
        return jnp.einsum("qhd,khd->hqk", q, key_seg, preferred_element_type=F32) * scale + extra

    def forward(carry, k):
        best, mass, acc = carry
        value = score(k, all_keys[k])
        new = jnp.maximum(best, jnp.max(value, axis=-1, keepdims=True))
        shrink = jnp.exp(best - new)
        weight = jnp.where(value > 0.5 * NEG, jnp.exp(value - new), 0.0)
        acc = acc * shrink + jnp.einsum(
            "hqk,khd->hqd", weight.astype(BF16), all_values[k], preferred_element_type=F32
        )
        return (new, mass * shrink + jnp.sum(weight, axis=-1, keepdims=True), acc), None

    start = (
        jnp.full((heads, seg_len, 1), NEG, F32),
        jnp.zeros((heads, seg_len, 1), F32),
        jnp.zeros((heads, seg_len, hd), F32),
    )
    order = jnp.arange(seq_count, dtype=jnp.int32)
    (best, mass, acc), _ = lax.scan(forward, start, order)
    attended = acc / mass
    lse = best + jnp.log(mass)
    delta = jnp.sum(attended * g.astype(F32).transpose(1, 0, 2), axis=-1, keepdims=True)

    def backward(dq, k):
        prob = jnp.exp(score(k, all_keys[k]) - lse)
        dprob = jnp.einsum("qhd,khd->hqk", g, all_values[k], preferred_element_type=F32)
        dscore = (prob * (dprob - delta) * scale).astype(BF16)
        dq = dq + jnp.einsum("hqk,khd->hqd", dscore, all_keys[k], preferred_element_type=F32)
        dk = jnp.einsum("hqk,qhd->khd", dscore, q, preferred_element_type=F32)
        dv = jnp.einsum("hqk,qhd->khd", prob.astype(BF16), g, preferred_element_type=F32)
        return dq, (dk.reshape(seg_len, features), dv.reshape(seg_len, features))

    dq, (dk, dv) = lax.scan(backward, jnp.zeros((heads, seg_len, hd), F32), order)
    dk = lax.psum_scatter(dk, "seq", scatter_dimension=0)
    dv = lax.psum_scatter(dv, "seq", scatter_dimension=0)

    def rows(x):
        return x.transpose(1, 0, 2).reshape(seg_len, features).astype(BF16)

    return rows(attended), rows(dq), dk.astype(BF16), dv.astype(BF16)


def shards(queries, keys, values, grad_out, retrieved, mem_bias):
    heads = mem_bias.shape[0]
    hd = keys.shape[1] // heads
    if (
        lax.axis_size("seq") == 2 * heads
        and hd % 128 == 0
        and retrieved.shape[0] <= 8
        and heads > 1
        and lax.axis_size("head") > 1
    ):
        return by_heads(queries, keys, values, grad_out, retrieved, mem_bias)
    return by_segments(queries, keys, values, grad_out, retrieved, mem_bias)


def solution(mesh):
    placed = (
        P("seq", "head"),
        P("seq", "head"),
        P("seq", "head"),
        P("seq", "head"),
        P(("seq", "head"), None),
        P("head"),
    )
    return jax.shard_map(
        shards,
        mesh=mesh,
        in_specs=placed,
        out_specs=(P("seq", "head"), P("seq", "head"), P("seq", "head"), P("seq", "head")),
        check_vma=False,
    )
```
